32 devices in a mesh: depth: 16 (over z, x, core), azi: 2 (over y).
Axes of the slice: x: 2, y: 2, z: 4, core: 2. Of those that a mesh axis runs over, the one named last changes fastest.
Arguments:
- heat_state: float32 [256, 128, 1024], P('depth', None, 'azi'), may hold values from -6 to 6
- tangent_in: float32 [256, 128, 1024], P('depth', None, 'azi'), may hold values from -6 to 6
- cotangent: float32 [256, 128, 1024], P('depth', None, 'azi'), may hold values from -6 to 6
- wet_mask: int32 [256, 1024], P('depth', 'azi'), may hold values 0 or 1
- sensors: int32 [256, 1024], P('depth', 'azi'), may hold values from 0 to 127
- propagators: bfloat16 [1024, 128, 128], P('azi', 'depth'), as said below
Outputs:
- new_state: bfloat16 [256, 128, 1024], P('depth', None, 'azi')
- tangent_out: bfloat16 [256, 128, 1024], P('depth', None, 'azi')
- gradient: float32 [256, 128, 1024], P('depth', None, 'azi')
- readings: bfloat16 [256, 1024], P('depth', 'azi')
The draws below stay inside these ranges and needn't reach their ends.
Inputs may be any that keep to these rules, and one draw needn't show every extreme that they name: `propagators`: each mode's radial propagator has diagonal entries between 0.55 and 1 and off-diagonal entries of magnitude at most 1.4 / sqrt(128).
All inputs are finite; a program needn't handle non-finite values. No bound on the sum of `wet_mask` on one device may be relied on, other than what follows from the above.
Results may differ from the reference program's by a relative error of at most 0.0078.
Values may be sent and summed in bfloat16 or wider, within the bound.
A program may use at most 128 MiB of HBM per device.

```python
import math
import jax
import jax.numpy as jnp
from jax import lax

A = 1024
R = 128
Z = 256


def draw_propagators(key, part):
    diag_key = jax.random.fold_in(key, 11)
    off_key = jax.random.fold_in(key, 23)
    diagonal = jax.random.uniform(diag_key, (A, R, 1), jnp.float32, 0.55, 1.0)
    spread = 0.35 / R ** 0.5
    off_diag = jnp.clip(jax.random.normal(off_key, (A, R, R), jnp.float32), -4.0, 4.0) * spread
    row_index = jnp.arange(R, dtype=jnp.int32)[None, :, None]
    col_index = jnp.arange(R, dtype=jnp.int32)[None, None, :]
    return jnp.where(row_index == col_index, diagonal, off_diag).astype(jnp.bfloat16)


def place_ends(values, key, least, top_value):
    extent = values.shape
    index_at = [jax.random.randint(jax.random.fold_in(key, axis), (), 0, extent[axis]) for axis in range(len(extent))]
    values = values.at[tuple(index_at)].set(least)
    longest = extent.index(max(extent))
    index_at[longest] = (index_at[longest] + 1) % extent[longest]
    return values.at[tuple(index_at)].set(top_value)


def levels(own_key, extent, pieces, least, high):
    def one(axis_at, parts):
        heights = jax.random.uniform(jax.random.fold_in(jax.random.fold_in(own_key, 6), axis_at), (parts,), jnp.float32, least / len(pieces), high / len(pieces))
        return jnp.repeat(jnp.exp(heights), extent[axis_at] // parts).reshape((-1,) + (1,) * (len(extent) - axis_at - 1))

    level = one(*pieces[0])
    for cut in pieces[1:]:
        level = level * one(*cut)
    return level


def bell_draw(own_key, shape, scale, bound, cuts=(), held_as=jnp.bfloat16):
    entries = jax.random.normal(own_key, shape, jnp.float32) * scale
    if len(cuts) > 0:
        entries = levels(own_key, shape, cuts, -0.22, 0.18) * entries
    return jnp.clip(entries, min=-bound, max=bound).astype(held_as)


def setup_inputs(seed: int = 0) -> dict:
    seeds = jax.random.split(jax.random.key(seed), 7)
    heat_state = bell_draw(seeds[0], (Z, R, A), 1.0, 6.0, ((0, 16), (2, 2)), jnp.float32)
    tangent_in = bell_draw(seeds[1], (Z, R, A), 1.0, 6.0, ((0, 16), (2, 2)), jnp.float32)
    cotangent = bell_draw(seeds[2], (Z, R, A), 1.0, 6.0, ((0, 16), (2, 2)), jnp.float32)
    wet_mask = place_ends((jax.random.randint(seeds[3], (Z, A), 0, 2) < 1).astype(jnp.int32), jax.random.fold_in(seeds[3], 1), 0, 1)
    sensors = place_ends(jax.random.randint(seeds[4], (Z, A), 0, R), jax.random.fold_in(seeds[4], 1), 0, R - 1).astype(jnp.int32)
    propagators = draw_propagators(jax.random.fold_in(seeds[6], 71), 0)
    return {"heat_state": heat_state, "tangent_in": tangent_in, "cotangent": cotangent, "wet_mask": wet_mask, "sensors": sensors, "propagators": propagators}


mixing = 0.25
evaporation = 0.6
skin_depth = 16.0

def fourier_table(length):
    wavenumber = jnp.arange(length, dtype=jnp.int32)[:, None]
    position = jnp.arange(length, dtype=jnp.int32)[None, :]
    midpoint = length // 2
    harmonic = jnp.where(wavenumber <= midpoint, wavenumber, wavenumber - midpoint)
    phase_angle = (harmonic * position % length).astype(jnp.float32) * (2.0 * math.pi / length)
    waveform = jnp.where(wavenumber <= midpoint, jnp.cos(phase_angle), jnp.sin(phase_angle))
    boundary_rows = (wavenumber == 0) | (wavenumber == midpoint)
    weights = jnp.where(boundary_rows, math.sqrt(1.0 / length), math.sqrt(2.0 / length))
    return (waveform * weights).astype(jnp.bfloat16)

def depth_mix(field):
    padded = jnp.pad(field, ((1, 1), (0, 0), (0, 0)))
    return padded[2:] + padded[:-2] - 2.0 * field

def reference(heat_state, tangent_in, cotangent, wet_mask, sensors, propagators):
    fourier = fourier_table(A).astype(jnp.float32)
    prop_full = propagators.astype(jnp.float32)
    profile = jnp.exp(-jnp.arange(R).astype(jnp.float32) / skin_depth)[None, :, None]
    damping = evaporation * wet_mask.astype(jnp.float32)[:, None, :] * profile
    moisture = jnp.tanh(heat_state)
    slope = 1.0 - moisture * moisture
    forward_rhs = (heat_state + mixing * depth_mix(heat_state) - damping * moisture).astype(jnp.bfloat16)
    tangent_rhs = (tangent_in + mixing * depth_mix(tangent_in) - damping * slope * tangent_in).astype(jnp.bfloat16)
    adjoint_seed = cotangent.astype(jnp.bfloat16)
    block = math.gcd(Z, 8)
    highest = lax.Precision.HIGHEST

    def spectral(fields, flipped):
        grouped = fields.reshape(Z // block, block, R, A)

        def one_block(piece):
            spectrum = jnp.einsum('ka,zra->zrk', fourier, piece.astype(jnp.float32), precision=highest).astype(jnp.bfloat16)
            if flipped:
                solved = jnp.einsum('ksr,zsk->zrk', prop_full, spectrum.astype(jnp.float32), precision=highest)
            else:
                solved = jnp.einsum('krs,zsk->zrk', prop_full, spectrum.astype(jnp.float32), precision=highest)
            solved = solved.astype(jnp.bfloat16)
            return jnp.einsum('ka,zrk->zra', fourier, solved.astype(jnp.float32), precision=highest).astype(jnp.bfloat16)
        return lax.map(one_block, grouped).reshape(Z, R, A)
    new_state = spectral(forward_rhs, False)
    tangent_out = spectral(tangent_rhs, False)
    dual = spectral(adjoint_seed, True).astype(jnp.float32)
    gradient = dual + mixing * depth_mix(dual) - damping * slope * dual
    readings = jnp.take_along_axis(new_state, sensors[:, None, :].astype(jnp.int32), axis=1)[:, 0, :]
    return (new_state, tangent_out, gradient, readings)
```

```python
import math

import jax
import jax.numpy as jnp
import numpy as np
from jax import lax
from jax.experimental import pallas as pl
from jax.sharding import PartitionSpec as P

mixing = 0.25
evaporation = 0.6
skin_depth = 16.0
mode_chunks = 2


def halo_planes(value):
    size = lax.axis_size("depth")
    up = [(i, i + 1) for i in range(size - 1)]
    down = [(j, i) for i, j in up]
    before = lax.ppermute(value[-1:], "depth", up)
    after = lax.ppermute(value[:1], "depth", down)
    return before, after


def damping_profile(rows, lanes):
    radius = pl.program_id(0) * rows + lax.broadcasted_iota(jnp.int32, (rows, lanes), 0)
    return evaporation * jnp.exp(-radius.astype(jnp.float32) / skin_depth)


def plane(ref, before, after, z):
    source, index = (before, 0) if z < 0 else (after, 0) if z == ref.shape[0] else (ref, z)
    return source[index].astype(jnp.float32)


def mixed(ref, before, after, z):
    centre = plane(ref, before, after, z)
    around = plane(ref, before, after, z + 1) + plane(ref, before, after, z - 1)
    return centre, centre + mixing * (around - 2.0 * centre)


def rhs_kernel(wet, heat, heat_before, heat_after, tangent, tangent_before, tangent_after, out, tangent_out):
    slab, rows, lanes = heat.shape
    profile = damping_profile(rows, lanes)
    for z in range(slab):
        damping = wet[z : z + 1].astype(jnp.float32) * profile
        centre, value = mixed(heat, heat_before, heat_after, z)
        moisture = jnp.tanh(centre)
        out[z] = (value - damping * moisture).astype(out.dtype)
        slope = 1.0 - moisture * moisture
        centre, value = mixed(tangent, tangent_before, tangent_after, z)
        tangent_out[z] = (value - damping * slope * centre).astype(tangent_out.dtype)


def gradient_kernel(wet, heat, dual, dual_before, dual_after, out):
    slab, rows, lanes = heat.shape
    profile = damping_profile(rows, lanes)
    for z in range(slab):
        damping = wet[z : z + 1].astype(jnp.float32) * profile
        moisture = jnp.tanh(heat[z])
        slope = 1.0 - moisture * moisture
        centre, value = mixed(dual, dual_before, dual_after, z)
        out[z] = value - damping * slope * centre


def by_radius(kernel, wet, fields, dtypes):
    slab, radial, lanes = fields[0].shape
    rows = min(radial, 16)

    def spec(depth):
        return pl.BlockSpec((depth, rows, lanes), lambda i: (0, i, 0))

    count = len(dtypes) * slab * radial * lanes
    return pl.pallas_call(
        kernel,
        grid=(radial // rows,),
        in_specs=[pl.BlockSpec(wet.shape, lambda i: (0, 0))] + [spec(f.shape[0]) for f in fields],
        out_specs=[spec(slab) for _ in dtypes],
        out_shape=[jax.ShapeDtypeStruct((slab, radial, lanes), dtype) for dtype in dtypes],
        cost_estimate=pl.CostEstimate(flops=10 * count, bytes_accessed=6 * count, transcendentals=count),
    )(wet, *fields)


def fourier_table(length):
    wavenumber = np.arange(length, dtype=np.int32)[:, None]
    position = np.arange(length, dtype=np.int32)[None, :]
    midpoint = length // 2
    harmonic = np.where(wavenumber <= midpoint, wavenumber, wavenumber - midpoint)
    phase = (harmonic * position % length).astype(np.float32) * np.float32(2.0 * math.pi / length)
    waveform = np.where(wavenumber <= midpoint, np.cos(phase), np.sin(phase))
    boundary = (wavenumber == 0) | (wavenumber == midpoint)
    weights = np.where(boundary, math.sqrt(1.0 / length), math.sqrt(2.0 / length)).astype(np.float32)
    return (waveform * weights).astype(jnp.bfloat16)


def from_all(value):
    size = lax.axis_size("azi")
    blocks = [value]
    for shift in range(1, size):
        pairs = [(i, (i + shift) % size) for i in range(size)]
        blocks.append(lax.ppermute(value, "azi", pairs))
    return blocks


def body(table, heat_state, tangent_in, cotangent, wet_mask, sensors, propagators):
    slab, radial, local_azi = heat_state.shape
    size = lax.axis_size("azi")
    me = lax.axis_index("azi")
    owners = [lax.rem(me - shift + size, size) for shift in range(size)]
    modes = propagators.shape[0]
    step = modes // mode_chunks

    whole = [
        lax.all_gather(propagators[c * step : (c + 1) * step], "depth", axis=1, tiled=True)
        for c in range(mode_chunks)
    ]

    seed_blocks = from_all(cotangent.astype(jnp.bfloat16))

    forward_rhs, tangent_rhs = by_radius(
        rhs_kernel,
        wet_mask,
        [heat_state, *halo_planes(heat_state), tangent_in, *halo_planes(tangent_in)],
        [jnp.bfloat16] * 2,
    )
    own_seed, forward_rhs, tangent_rhs = lax.optimization_barrier(
        (seed_blocks[0], forward_rhs, tangent_rhs)
    )
    seed_blocks = [own_seed] + seed_blocks[1:]
    forward_blocks = from_all(forward_rhs)
    tangent_blocks = from_all(tangent_rhs)

    own_modes = lax.dynamic_slice_in_dim(table, me * modes, modes, axis=0)
    to_modes = [
        lax.dynamic_slice_in_dim(own_modes, owner * local_azi, local_azi, axis=1) for owner in owners
    ]
    own_azimuths = lax.dynamic_slice_in_dim(table, me * local_azi, local_azi, axis=1)
    to_azimuths = [
        lax.dynamic_slice_in_dim(own_azimuths, owner * modes, modes, axis=0) for owner in owners
    ]

    def solve(blocks, formula):
        returned = []
        for c in range(mode_chunks):
            rows = slice(c * step, (c + 1) * step)
            total = 0.0
            for weights, block in zip(to_modes, blocks):
                total = total + jnp.einsum(
                    "ka,zra->kzr", weights[rows], block, preferred_element_type=jnp.float32
                )
            solved = jnp.einsum(
                formula, whole[c], total.astype(jnp.bfloat16), preferred_element_type=jnp.float32
            ).astype(jnp.bfloat16)
            returned.append(from_all(solved))
        return returned

    def inverse(returned):
        total = 0.0
        for c in range(mode_chunks):
            rows = slice(c * step, (c + 1) * step)
            for weights, block in zip(to_azimuths, returned[c]):
                total = total + jnp.einsum(
                    "ka,kzr->zra", weights[rows], block, preferred_element_type=jnp.float32
                )
        return total.astype(jnp.bfloat16)

    dual_modes = solve(seed_blocks, "ksr,kzs->kzr")
    forward_modes = solve(forward_blocks, "krs,kzs->kzr")
    tangent_modes = solve(tangent_blocks, "krs,kzs->kzr")

    dual = inverse(dual_modes)
    (gradient,) = by_radius(
        gradient_kernel, wet_mask, [heat_state, dual, *halo_planes(dual)], [jnp.float32]
    )

    new_state = inverse(forward_modes)
    radial_index = jnp.arange(radial, dtype=jnp.int32)[None, :, None]
    selected = jnp.where(radial_index == sensors[:, None, :], new_state, jnp.zeros_like(new_state))
    readings = jnp.sum(selected, axis=1)

    tangent_out = inverse(tangent_modes)
    return (new_state, tangent_out, gradient, readings)


def solution(mesh):
    def run(heat_state, tangent_in, cotangent, wet_mask, sensors, propagators):
        table = jnp.asarray(fourier_table(heat_state.shape[2]))
        field = P("depth", None, "azi")
        panel = P("depth", "azi")
        return jax.shard_map(
            body,
            mesh=mesh,
            in_specs=(P(), field, field, field, panel, panel, P("azi", "depth", None)),
            out_specs=(field, field, field, panel),
            check_vma=False,
        )(table, heat_state, tangent_in, cotangent, wet_mask, sensors, propagators)

    return run
```

```python
import math

import jax
import jax.numpy as jnp
import numpy as np
from jax import lax
from jax.experimental import pallas as pl
from jax.sharding import PartitionSpec as P

mixing = 0.25
evaporation = 0.6
skin_depth = 16.0
mode_chunks = 2


def halo_planes(last, first):
    size = lax.axis_size("depth")
    up = [(i, i + 1) for i in range(size - 1)]
    down = [(j, i) for i, j in up]
    before = lax.ppermute(last, "depth", up)
    after = lax.ppermute(first, "depth", down)
    return before, after


def damping_profile(rows, lanes):
    radius = pl.program_id(0) * rows + lax.broadcasted_iota(jnp.int32, (rows, lanes), 0)
    return evaporation * jnp.exp(-radius.astype(jnp.float32) / skin_depth)


def plane(ref, before, after, z):
    source, index = (before, 0) if z < 0 else (after, 0) if z == ref.shape[0] else (ref, z)
    return source[index].astype(jnp.float32)


def mixed(ref, before, after, z):
    centre = plane(ref, before, after, z)
    around = plane(ref, before, after, z + 1) + plane(ref, before, after, z - 1)
    return centre, centre + mixing * (around - 2.0 * centre)


def rhs_kernel(wet, heat, heat_before, heat_after, tangent, tangent_before, tangent_after, out, tangent_out):
    slab, rows, lanes = heat.shape
    profile = damping_profile(rows, lanes)
    for z in range(slab):
        damping = wet[z : z + 1].astype(jnp.float32) * profile
        centre, value = mixed(heat, heat_before, heat_after, z)
        moisture = jnp.tanh(centre)
        out[z] = (value - damping * moisture).astype(out.dtype)
        slope = 1.0 - moisture * moisture
        centre, value = mixed(tangent, tangent_before, tangent_after, z)
        tangent_out[z] = (value - damping * slope * centre).astype(tangent_out.dtype)


def gradient_kernel(wet, heat, dual, dual_before, dual_after, out):
    slab, rows, lanes = heat.shape
    profile = damping_profile(rows, lanes)
    for z in range(slab):
        damping = wet[z : z + 1].astype(jnp.float32) * profile
        moisture = jnp.tanh(heat[z])
        slope = 1.0 - moisture * moisture
        centre, value = mixed(dual, dual_before, dual_after, z)
        out[z] = value - damping * slope * centre


def by_radius(kernel, wet, fields, dtypes):
    slab, radial, lanes = fields[0].shape
    rows = min(radial, 16)

    def spec(depth):
        return pl.BlockSpec((depth, rows, lanes), lambda i: (0, i, 0))

    count = len(dtypes) * slab * radial * lanes
    return pl.pallas_call(
        kernel,
        grid=(radial // rows,),
        in_specs=[pl.BlockSpec(wet.shape, lambda i: (0, 0))] + [spec(f.shape[0]) for f in fields],
        out_specs=[spec(slab) for _ in dtypes],
        out_shape=[jax.ShapeDtypeStruct((slab, radial, lanes), dtype) for dtype in dtypes],
        cost_estimate=pl.CostEstimate(flops=10 * count, bytes_accessed=6 * count, transcendentals=count),
    )(wet, *fields)


def fourier_table(length):
    wavenumber = np.arange(length, dtype=np.int32)[:, None]
    position = np.arange(length, dtype=np.int32)[None, :]
    midpoint = length // 2
    harmonic = np.where(wavenumber <= midpoint, wavenumber, wavenumber - midpoint)
    phase = (harmonic * position % length).astype(np.float32) * np.float32(2.0 * math.pi / length)
    waveform = np.where(wavenumber <= midpoint, np.cos(phase), np.sin(phase))
    boundary = (wavenumber == 0) | (wavenumber == midpoint)
    weights = np.where(boundary, math.sqrt(1.0 / length), math.sqrt(2.0 / length)).astype(np.float32)
    return (waveform * weights).astype(jnp.bfloat16)


def from_all(value):
    size = lax.axis_size("azi")
    blocks = [value]
    for shift in range(1, size):
        pairs = [(i, (i + shift) % size) for i in range(size)]
        blocks.append(lax.ppermute(value, "azi", pairs))
    return blocks


def body(table, heat_state, tangent_in, cotangent, wet_mask, sensors, propagators):
    slab, radial, local_azi = heat_state.shape
    size = lax.axis_size("azi")
    me = lax.axis_index("azi")
    owners = [lax.rem(me - shift + size, size) for shift in range(size)]
    modes = propagators.shape[0]
    step = modes // mode_chunks

    whole = [
        lax.all_gather(propagators[c * step : (c + 1) * step], "depth", axis=1, tiled=True)
        for c in range(mode_chunks)
    ]

    seed = cotangent.astype(jnp.bfloat16)
    seed, heat_last, heat_first, tangent_last, tangent_first = lax.optimization_barrier(
        (seed, heat_state[-1:], heat_state[:1], tangent_in[-1:], tangent_in[:1])
    )
    seed_blocks = from_all(seed)

    forward_rhs, tangent_rhs = by_radius(
        rhs_kernel,
        wet_mask,
        [heat_state, *halo_planes(heat_last, heat_first), tangent_in, *halo_planes(tangent_last, tangent_first)],
        [jnp.bfloat16] * 2,
    )
    own_seed, forward_rhs, tangent_rhs = lax.optimization_barrier(
        (seed_blocks[0], forward_rhs, tangent_rhs)
    )
    seed_blocks = [own_seed] + seed_blocks[1:]
    forward_blocks = from_all(forward_rhs)
    tangent_blocks = from_all(tangent_rhs)

    own_modes = lax.dynamic_slice_in_dim(table, me * modes, modes, axis=0)
    to_modes = [
        lax.dynamic_slice_in_dim(own_modes, owner * local_azi, local_azi, axis=1) for owner in owners
    ]
    own_azimuths = lax.dynamic_slice_in_dim(table, me * local_azi, local_azi, axis=1)
    to_azimuths = [
        lax.dynamic_slice_in_dim(own_azimuths, owner * modes, modes, axis=0) for owner in owners
    ]

    def solve(blocks, formula):
        returned = []
        for c in range(mode_chunks):
            rows = slice(c * step, (c + 1) * step)
            total = 0.0
            for weights, block in zip(to_modes, blocks):
                total = total + jnp.einsum(
                    "ka,zra->kzr", weights[rows], block, preferred_element_type=jnp.float32
                )
            solved = jnp.einsum(
                formula, whole[c], total.astype(jnp.bfloat16), preferred_element_type=jnp.float32
            ).astype(jnp.bfloat16)
            returned.append(from_all(solved))
        return returned

    def inverse(returned):
        total = 0.0
        for c in range(mode_chunks):
            rows = slice(c * step, (c + 1) * step)
            for weights, block in zip(to_azimuths, returned[c]):
                total = total + jnp.einsum(
                    "ka,kzr->zra", weights[rows], block, preferred_element_type=jnp.float32
                )
        return total.astype(jnp.bfloat16)

    dual_modes = solve(seed_blocks, "ksr,kzs->kzr")
    dual_modes[0][0], *forward_received = lax.optimization_barrier(
        (dual_modes[0][0], *forward_blocks[1:])
    )
    forward_blocks = forward_blocks[:1] + forward_received
    forward_modes = solve(forward_blocks, "krs,kzs->kzr")
    tangent_modes = solve(tangent_blocks, "krs,kzs->kzr")

    dual = inverse(dual_modes)
    (gradient,) = by_radius(
        gradient_kernel, wet_mask, [heat_state, dual, *halo_planes(dual[-1:], dual[:1])], [jnp.float32]
    )

    new_state = inverse(forward_modes)
    radial_index = jnp.arange(radial, dtype=jnp.int32)[None, :, None]
    selected = jnp.where(radial_index == sensors[:, None, :], new_state, jnp.zeros_like(new_state))
    readings = jnp.sum(selected, axis=1)

    gradient, *last_received = lax.optimization_barrier((gradient, *tangent_modes[-1][1:]))
    tangent_modes[-1] = tangent_modes[-1][:1] + last_received
    tangent_out = inverse(tangent_modes)
    return (new_state, tangent_out, gradient, readings)


def solution(mesh):
    def run(heat_state, tangent_in, cotangent, wet_mask, sensors, propagators):
        table = jnp.asarray(fourier_table(heat_state.shape[2]))
        field = P("depth", None, "azi")
        panel = P("depth", "azi")
        return jax.shard_map(
            body,
            mesh=mesh,
            in_specs=(P(), field, field, field, panel, panel, P("azi", "depth", None)),
            out_specs=(field, field, field, panel),
            check_vma=False,
        )(table, heat_state, tangent_in, cotangent, wet_mask, sensors, propagators)

    return run
```

```python
import math

import jax
import jax.numpy as jnp
import numpy as np
from jax import lax
from jax.experimental import pallas as pl
from jax.sharding import PartitionSpec as P

mixing = 0.25
evaporation = 0.6
skin_depth = 16.0
mode_chunks = 2


def halo_planes(last, first):
    size = lax.axis_size("depth")
    up = [(i, i + 1) for i in range(size - 1)]
    down = [(j, i) for i, j in up]
    before = lax.ppermute(last, "depth", up)
    after = lax.ppermute(first, "depth", down)
    return before, after


def damping_profile(rows, lanes):
    radius = pl.program_id(0) * rows + lax.broadcasted_iota(jnp.int32, (rows, lanes), 0)
    return evaporation * jnp.exp(-radius.astype(jnp.float32) / skin_depth)


def plane(ref, before, after, z):
    source, index = (before, 0) if z < 0 else (after, 0) if z == ref.shape[0] else (ref, z)
    return source[index].astype(jnp.float32)


def mixed(ref, before, after, z):
    centre = plane(ref, before, after, z)
    around = plane(ref, before, after, z + 1) + plane(ref, before, after, z - 1)
    return centre, centre + mixing * (around - 2.0 * centre)


def rhs_kernel(wet, heat, heat_before, heat_after, tangent, tangent_before, tangent_after, out, tangent_out):
    slab, rows, lanes = heat.shape
    profile = damping_profile(rows, lanes)
    for z in range(slab):
        damping = wet[z : z + 1].astype(jnp.float32) * profile
        centre, value = mixed(heat, heat_before, heat_after, z)
        moisture = jnp.tanh(centre)
        out[z] = (value - damping * moisture).astype(out.dtype)
        slope = 1.0 - moisture * moisture
        centre, value = mixed(tangent, tangent_before, tangent_after, z)
        tangent_out[z] = (value - damping * slope * centre).astype(tangent_out.dtype)


def gradient_kernel(wet, heat, dual, dual_before, dual_after, out):
    slab, rows, lanes = heat.shape
    profile = damping_profile(rows, lanes)
    for z in range(slab):
        damping = wet[z : z + 1].astype(jnp.float32) * profile
        moisture = jnp.tanh(heat[z])
        slope = 1.0 - moisture * moisture
        centre, value = mixed(dual, dual_before, dual_after, z)
        out[z] = value - damping * slope * centre


def by_radius(kernel, wet, fields, dtypes):
    slab, radial, lanes = fields[0].shape
    rows = min(radial, 16)

    def spec(depth):
        return pl.BlockSpec((depth, rows, lanes), lambda i: (0, i, 0))

    count = len(dtypes) * slab * radial * lanes
    return pl.pallas_call(
        kernel,
        grid=(radial // rows,),
        in_specs=[pl.BlockSpec(wet.shape, lambda i: (0, 0))] + [spec(f.shape[0]) for f in fields],
        out_specs=[spec(slab) for _ in dtypes],
        out_shape=[jax.ShapeDtypeStruct((slab, radial, lanes), dtype) for dtype in dtypes],
        cost_estimate=pl.CostEstimate(flops=10 * count, bytes_accessed=6 * count, transcendentals=count),
    )(wet, *fields)


def fourier_table(length):
    wavenumber = np.arange(length, dtype=np.int32)[:, None]
    position = np.arange(length, dtype=np.int32)[None, :]
    midpoint = length // 2
    harmonic = np.where(wavenumber <= midpoint, wavenumber, wavenumber - midpoint)
    phase = (harmonic * position % length).astype(np.float32) * np.float32(2.0 * math.pi / length)
    waveform = np.where(wavenumber <= midpoint, np.cos(phase), np.sin(phase))
    boundary = (wavenumber == 0) | (wavenumber == midpoint)
    weights = np.where(boundary, math.sqrt(1.0 / length), math.sqrt(2.0 / length)).astype(np.float32)
    return (waveform * weights).astype(jnp.bfloat16)


def from_all(value):
    size = lax.axis_size("azi")
    blocks = [value]
    for shift in range(1, size):
        pairs = [(i, (i + shift) % size) for i in range(size)]
        blocks.append(lax.ppermute(value, "azi", pairs))
    return blocks


def body(table, heat_state, tangent_in, cotangent, wet_mask, sensors, propagators):
    slab, radial, local_azi = heat_state.shape
    size = lax.axis_size("azi")
    me = lax.axis_index("azi")
    owners = [lax.rem(me - shift + size, size) for shift in range(size)]
    modes = propagators.shape[0]
    step = modes // mode_chunks

    whole = [
        lax.all_gather(propagators[c * step : (c + 1) * step], "depth", axis=1, tiled=True)
        for c in range(mode_chunks)
    ]

    own_modes = lax.dynamic_slice_in_dim(table, me * modes, modes, axis=0)
    to_modes = [
        lax.dynamic_slice_in_dim(own_modes, owner * local_azi, local_azi, axis=1) for owner in owners
    ]
    own_azimuths = lax.dynamic_slice_in_dim(table, me * local_azi, local_azi, axis=1)
    to_azimuths = [
        lax.dynamic_slice_in_dim(own_azimuths, owner * modes, modes, axis=0) for owner in owners
    ]

    def part_spectrum(weights, block, c):
        return jnp.einsum(
            "ka,zra->kzr",
            weights[c * step : (c + 1) * step],
            block,
            preferred_element_type=jnp.float32,
        )

    seed_blocks = from_all(cotangent.astype(jnp.bfloat16))
    seed_part, heat_last, heat_first, tangent_last, tangent_first = lax.optimization_barrier(
        (
            part_spectrum(to_modes[0], seed_blocks[0], 0),
            heat_state[-1:],
            heat_state[:1],
            tangent_in[-1:],
            tangent_in[:1],
        )
    )

    forward_rhs, tangent_rhs = by_radius(
        rhs_kernel,
        wet_mask,
        [heat_state, *halo_planes(heat_last, heat_first), tangent_in, *halo_planes(tangent_last, tangent_first)],
        [jnp.bfloat16] * 2,
    )
    own_seed, forward_rhs, tangent_rhs = lax.optimization_barrier(
        (seed_blocks[0], forward_rhs, tangent_rhs)
    )
    seed_blocks = [own_seed] + seed_blocks[1:]
    forward_blocks = from_all(forward_rhs)
    tangent_blocks = from_all(tangent_rhs)

    def solve(blocks, formula, first=None):
        returned = []
        for c in range(mode_chunks):
            known = c == 0 and first is not None
            total = first if known else part_spectrum(to_modes[0], blocks[0], c)
            for weights, block in zip(to_modes[1:], blocks[1:]):
                total = total + part_spectrum(weights, block, c)
            solved = jnp.einsum(
                formula, whole[c], total.astype(jnp.bfloat16), preferred_element_type=jnp.float32
            ).astype(jnp.bfloat16)
            returned.append(from_all(solved))
        return returned

    def part_inverse(returned, pairs):
        total = 0.0
        for c, i in pairs:
            total = total + jnp.einsum(
                "ka,kzr->zra",
                to_azimuths[i][c * step : (c + 1) * step],
                returned[c][i],
                preferred_element_type=jnp.float32,
            )
        return total

    pairs = [(c, i) for i in range(size) for c in range(mode_chunks)]

    def inverse(returned):
        return part_inverse(returned, pairs).astype(jnp.bfloat16)

    dual_modes = solve(seed_blocks, "ksr,kzs->kzr", seed_part)
    dual_modes[0][0], *forward_received = lax.optimization_barrier(
        (dual_modes[0][0], *forward_blocks[1:])
    )
    forward_blocks = forward_blocks[:1] + forward_received
    forward_modes = solve(forward_blocks, "krs,kzs->kzr")
    tangent_modes = solve(tangent_blocks, "krs,kzs->kzr")

    dual = inverse(dual_modes)
    (gradient,) = by_radius(
        gradient_kernel, wet_mask, [heat_state, dual, *halo_planes(dual[-1:], dual[:1])], [jnp.float32]
    )

    new_state = inverse(forward_modes)
    radial_index = jnp.arange(radial, dtype=jnp.int32)[None, :, None]
    selected = jnp.where(radial_index == sensors[:, None, :], new_state, jnp.zeros_like(new_state))
    readings = jnp.sum(selected, axis=1)

    partial = part_inverse(tangent_modes, pairs[:-1])
    gradient, partial, tangent_modes[-1][-1] = lax.optimization_barrier(
        (gradient, partial, tangent_modes[-1][-1])
    )
    tangent_out = (partial + part_inverse(tangent_modes, pairs[-1:])).astype(jnp.bfloat16)
    return (new_state, tangent_out, gradient, readings)


def solution(mesh):
    def run(heat_state, tangent_in, cotangent, wet_mask, sensors, propagators):
        table = jnp.asarray(fourier_table(heat_state.shape[2]))
        field = P("depth", None, "azi")
        panel = P("depth", "azi")
        return jax.shard_map(
            body,
            mesh=mesh,
            in_specs=(P(), field, field, field, panel, panel, P("azi", "depth", None)),
            out_specs=(field, field, field, panel),
            check_vma=False,
        )(table, heat_state, tangent_in, cotangent, wet_mask, sensors, propagators)

    return run
```
